32 devices in a mesh: tm: 8 (over z, y), scan: 4 (over x, core).
Axes of the slice: x: 2, y: 2, z: 4, core: 2. Of those that a mesh axis runs over, the one named last changes fastest.
Arguments:
- spec_grad: float32 [1, 2, 1048576], P(None, None, 'tm'), may hold values from -6 to 6
- transients: bfloat16 [1, 32, 1048576], P(None, 'scan', 'tm')
- kernels: float32 [16, 16], replicated, may hold values from -1.5 to 1.5
- shifts: int32 [1, 32], P(None, 'scan'), may hold values from -512 to 512, as said below
- tiles: int32 [1, 32], P(None, 'scan'), may hold values from 0 to 15
Outputs:
- scan_grad: float32 [1, 32, 1048576], P(None, 'scan', 'tm')
- kernel_grad: float32 [16, 16], replicated
The draws below stay inside these ranges and needn't reach their ends.
Inputs may be any that keep to these rules, and one draw needn't show every extreme that they name: `shifts`: in every window one scan has shift 512 and another has shift -512.
All inputs are finite; a program needn't handle non-finite values.
Results may differ from the reference program's by a relative error of at most 0.0003.
Values sent between devices are 32-bit elements; how exact they have to be, the bound alone decides.
A program may use at most 64 MiB of HBM per device.

```python
import jax
import jax.numpy as jnp
from jax import lax

N = 1048576
WIN = 1
SCANS = 32
TILES = 16
TAPS = 16
KMAX = 512


def draw_transients(key, part):
    key_noise = jax.random.fold_in(key, 11)
    key_amp = jax.random.fold_in(key, 12)
    noise = jax.random.normal(key_noise, (WIN, SCANS, N), jnp.float32)
    amp = jnp.exp(jax.random.uniform(key_amp, (WIN, SCANS, 1), jnp.float32, -0.7, 0.7))
    envelope = jnp.exp(-1.5 * jnp.arange(N, dtype=jnp.float32) / N)
    return (noise * amp * envelope[None, None, :] / 1024.0).astype(jnp.bfloat16)


def draw_shifts(key, part):
    first = jax.random.randint(jax.random.fold_in(key, 21), (WIN, SCANS), 0, KMAX + 1)
    second = jax.random.randint(jax.random.fold_in(key, 22), (WIN, SCANS), 0, KMAX + 1)
    sign = jax.random.randint(jax.random.fold_in(key, 23), (WIN, SCANS), 0, 2) * 2 - 1
    values = first * second // KMAX * sign
    top_pos = jax.random.randint(jax.random.fold_in(key, 24), (WIN,), 0, SCANS)
    low_pos = (top_pos + 1 + jax.random.randint(jax.random.fold_in(key, 25), (WIN,), 0, SCANS - 1)) % SCANS
    rows = jnp.arange(WIN)
    values = values.at[rows, top_pos].set(KMAX)
    values = values.at[rows, low_pos].set(-KMAX)
    return values.astype(jnp.int32)


def plant(array, stream_key, low, high):
    index_at = [jax.random.randint(jax.random.fold_in(stream_key, axis), (), 0, length) for axis, length in enumerate(array.shape)]
    longest = array.shape.index(max(array.shape))
    beside = index_at[:longest] + [(index_at[longest] + 1) % array.shape[longest]] + index_at[longest + 1:]
    return array.at[tuple(index_at)].set(low).at[tuple(beside)].set(high)


def shard_levels(key, shape, split, low, top_value):
    loudness = 1.0
    for axis_at, parts in split:
        heights = jax.random.uniform(jax.random.fold_in(jax.random.fold_in(key, 6), axis_at), (parts,), jnp.float32, low / len(split), top_value / len(split))
        loudness = loudness * jnp.repeat(jnp.exp(heights), shape[axis_at] // parts).reshape((-1,) + (1,) * (len(shape) - 1 - axis_at))
    return loudness


def bell_draw(stream_key, extent, spread, most, shards=(), kind=jnp.bfloat16):
    values = jax.random.normal(stream_key, extent, jnp.float32) * spread
    if len(shards) > 0:
        values = shard_levels(stream_key, extent, shards, -0.22, 0.18) * values
    return jnp.clip(values, min=-most, max=most).astype(kind)


def setup_inputs(seed: int = 0) -> dict:
    arg_keys = jax.random.split(jax.random.key(seed), 6)
    spec_grad = bell_draw(arg_keys[0], (WIN, 2, N), 1.0, 6.0, ((2, 8),), jnp.float32)
    transients = draw_transients(jax.random.fold_in(arg_keys[5], 71), 0)
    kernels = bell_draw(arg_keys[2], (TILES, TAPS), TAPS ** -0.5, 1.5, (), jnp.float32)
    shifts = draw_shifts(jax.random.fold_in(arg_keys[5], 71), 0)
    tiles = plant(jax.random.randint(arg_keys[4], (WIN, SCANS), 0, TILES), jax.random.fold_in(arg_keys[4], 1), 0, TILES - 1).astype(jnp.int32)
    return {"spec_grad": spec_grad, "transients": transients, "kernels": kernels, "shifts": shifts, "tiles": tiles}


def reference(spec_grad, transients, kernels, shifts, tiles):
    half = TAPS // 2
    width = KMAX + half
    spectrum = lax.complex(spec_grad[:, 0], spec_grad[:, 1])
    avg_grad = (jnp.real(jnp.fft.ifft(spectrum, axis=-1)) * (N ** 0.5)).astype(jnp.float32)
    padded = jnp.pad(avg_grad, ((0, 0), (width, width)))
    flat_x = transients.reshape(WIN * SCANS, N)
    flat_shift = shifts.reshape(WIN * SCANS).astype(jnp.int32)
    flat_win = (jnp.arange(WIN * SCANS) // SCANS).astype(jnp.int32)
    flat_taps = kernels[tiles.reshape(WIN * SCANS)]

    def one_scan(items):
        signal, shift, window, taps = items
        start = (width + half - shift - TAPS + 1).astype(jnp.int32)
        segment = lax.dynamic_slice_in_dim(padded[window], start, N + TAPS - 1)
        result = jnp.zeros((N,), jnp.float32)
        corr_list = []
        for j in range(TAPS):
            window_vals = segment[TAPS - 1 - j:TAPS - 1 - j + N]
            result = result + taps[j] * window_vals
            corr_list.append(jnp.sum(signal.astype(jnp.float32) * window_vals))
        return result, jnp.stack(corr_list)

    grads, corr = lax.map(one_scan, (flat_x, flat_shift, flat_win, flat_taps))
    onehot = (tiles.reshape(WIN * SCANS)[:, None] == jnp.arange(TILES)[None, :]).astype(jnp.float32)
    kernel_grad = jnp.dot(onehot.T, corr, precision=lax.Precision.HIGHEST, preferred_element_type=jnp.float32)
    return grads.reshape(WIN, SCANS, N), kernel_grad
```

```python
import functools
import math

import jax
import jax.numpy as jnp
from jax import lax
from jax.experimental import pallas as pl
from jax.experimental.pallas import tpu as pltpu
from jax.sharding import PartitionSpec as P

N1 = 1024
N2 = 1024
TILES = 16
TAPS = 16
KMAX = 512


highest = lax.Precision.HIGHEST
high = lax.Precision.HIGH
LANES = 128
EDGE = 5
MESH = pl.DeviceIdType.MESH


def halves(x):
    top = x.astype(jnp.bfloat16)
    return top, (x - top.astype(jnp.float32)).astype(jnp.bfloat16)


def fir_kernel(chunk, shifts_ref, tiles_ref, kernels_ref, g_ref, x_ref, out_ref, table_ref,
               gg, t_hi, t_lo, corr, xs, ys):
    step = pl.program_id(0)
    scans = x_ref.shape[0]
    rows = g_ref.shape[0] - 8

    def place(s):
        start = EDGE * LANES - TAPS // 2 + 1 - shifts_ref[s]
        return start // LANES, (start // (LANES // 2)) % 2, start % (LANES // 2)

    @pl.when(step == 0)
    def _():
        gg[0] = g_ref[:rows]
        lane = lax.broadcasted_iota(jnp.int32, (rows, LANES), 1)
        here = pltpu.roll(g_ref[:rows], LANES // 2, 1)
        nxt = pltpu.roll(g_ref[1 : rows + 1], LANES // 2, 1)
        gg[1] = jnp.where(lane < LANES // 2, here, nxt)
        row = lax.broadcasted_iota(jnp.int32, (2 * LANES, LANES), 0)
        col = lax.broadcasted_iota(jnp.int32, (2 * LANES, LANES), 1)

        def band(s, carry):
            _, _, o = place(s)
            tap = o + col + (TAPS - 1) - row
            value = jnp.zeros((2 * LANES, LANES), jnp.float32)
            for j in range(TAPS):
                value = jnp.where(tap == j, kernels_ref[tiles_ref[s], j], value)
            top, rest = halves(value)
            t_hi[s] = top
            t_lo[s] = rest
            corr[s] = jnp.zeros((LANES, 2 * LANES), jnp.float32)
            return carry

        lax.fori_loop(0, scans, band, 0)

    def split_in(r, carry):
        at = pl.ds(pl.multiple_of(r * LANES, LANES), LANES)
        xs[pl.ds(pl.multiple_of(r * scans, scans), scans), :] = x_ref[:, at].astype(jnp.float32)
        return carry

    lax.fori_loop(0, chunk, split_in, 0, unroll=8)

    for s in range(scans):
        q, c, _ = place(s)
        first = step * chunk + q
        window = jnp.concatenate(
            [gg[c, pl.ds(first, chunk), :], gg[c, pl.ds(first + 1, chunk), :]], axis=1
        )
        top, rest = halves(window)
        dot = functools.partial(jnp.dot, preferred_element_type=jnp.float32)
        ys[s * chunk : (s + 1) * chunk, :] = (
            dot(top, t_hi[s]) + (dot(top, t_lo[s]) + dot(rest, t_hi[s]))
        )
        x = xs[pl.ds(s, chunk, stride=scans), :].astype(jnp.bfloat16)
        down = functools.partial(
            lax.dot_general,
            dimension_numbers=(((0,), (0,)), ((), ())),
            preferred_element_type=jnp.float32,
        )
        corr[s] += down(x, top) + down(x, rest)

    def join_out(r, carry):
        at = pl.ds(pl.multiple_of(r * LANES, LANES), LANES)
        out_ref[:, at] = ys[pl.ds(r, scans, stride=chunk), :]
        return carry

    lax.fori_loop(0, chunk, join_out, 0, unroll=8)

    @pl.when(step == pl.num_programs(0) - 1)
    def _():
        apart = lax.broadcasted_iota(jnp.int32, (LANES, 2 * LANES), 1) - lax.broadcasted_iota(
            jnp.int32, (LANES, 2 * LANES), 0
        )
        tap = lax.broadcasted_iota(jnp.int32, (TAPS, LANES), 0)
        tile = lax.broadcasted_iota(jnp.int32, (TAPS, LANES), 1)

        def fold(s, total):
            _, _, o = place(s)
            values = corr[s]
            sums = [
                jnp.sum(jnp.where(apart == o + (TAPS - 1 - j), values, 0.0), axis=0, keepdims=True)
                for j in range(TAPS)
            ]
            column = jnp.sum(jnp.concatenate(sums, axis=0), axis=1, keepdims=True)
            return total + jnp.where(tile == tiles_ref[s], column, 0.0)

        table_ref[...] = lax.fori_loop(0, scans, fold, jnp.zeros((TAPS, LANES), jnp.float32))


def scans_and_table(padded_g, x, kernels, shifts, tiles):
    scans, stretch = x.shape
    rows = stretch // LANES
    chunk = min(256, rows)
    deep = padded_g.shape[0]
    smem = pl.BlockSpec(memory_space=pltpu.SMEM)
    return pl.pallas_call(
        functools.partial(fir_kernel, chunk),
        grid=(rows // chunk,),
        out_shape=[
            jax.ShapeDtypeStruct((scans, stretch), jnp.float32),
            jax.ShapeDtypeStruct((TAPS, LANES), jnp.float32),
        ],
        in_specs=[
            smem,
            smem,
            smem,
            pl.BlockSpec((deep, LANES), lambda i: (0, 0)),
            pl.BlockSpec((scans, chunk * LANES), lambda i: (0, i)),
        ],
        out_specs=[
            pl.BlockSpec((scans, chunk * LANES), lambda i: (0, i)),
            pl.BlockSpec((TAPS, LANES), lambda i: (0, 0)),
        ],
        scratch_shapes=[
            pltpu.VMEM((2, deep - 8, LANES), jnp.float32),
            pltpu.VMEM((scans, 2 * LANES, LANES), jnp.bfloat16),
            pltpu.VMEM((scans, 2 * LANES, LANES), jnp.bfloat16),
            pltpu.VMEM((scans, LANES, 2 * LANES), jnp.float32),
            pltpu.VMEM((scans * chunk, LANES), jnp.float32),
            pltpu.VMEM((scans * chunk, LANES), jnp.float32),
        ],
        compiler_params=pltpu.CompilerParams(vmem_limit_bytes=40 * 2**20),
        name="fir",
    )(shifts, tiles, kernels, padded_g, x)


def sum_kernel(sizes, in_ref, out_ref, first, second, send, recv, send2, recv2):
    here = [lax.axis_index("tm"), lax.axis_index("scan")]
    barrier = pltpu.get_barrier_semaphore()

    def peer(axis, k):
        other = list(here)
        other[axis] = lax.rem(here[axis] + k, sizes[axis])
        return tuple(other)

    for axis in range(2):
        for k in range(1, sizes[axis]):
            pl.semaphore_signal(barrier, inc=1, device_id=peer(axis, k), device_id_type=MESH)
    pl.semaphore_wait(barrier, sizes[0] + sizes[1] - 2)
    value = in_ref[...]
    for axis, slots, out_sem, in_sem in ((0, first, send, recv), (1, second, send2, recv2)):
        slots[here[axis]] = value
        copies = [
            pltpu.make_async_remote_copy(
                src_ref=slots.at[here[axis]],
                dst_ref=slots.at[here[axis]],
                send_sem=out_sem.at[k],
                recv_sem=in_sem.at[k],
                device_id=peer(axis, k),
                device_id_type=MESH,
            )
            for k in range(1, sizes[axis])
        ]
        for copy in copies:
            copy.start()
        for copy in copies:
            copy.wait()
        value = slots[0]
        for k in range(1, sizes[axis]):
            value = value + slots[k]
    out_ref[...] = value


def sum_everywhere(table, sizes):
    dma = pltpu.SemaphoreType.DMA
    vmem = pl.BlockSpec(memory_space=pltpu.VMEM)
    return pl.pallas_call(
        functools.partial(sum_kernel, sizes),
        out_shape=jax.ShapeDtypeStruct(table.shape, table.dtype),
        in_specs=[vmem],
        out_specs=vmem,
        scratch_shapes=[
            pltpu.VMEM((sizes[0],) + table.shape, table.dtype),
            pltpu.VMEM((sizes[1],) + table.shape, table.dtype),
            dma((sizes[0],)),
            dma((sizes[0],)),
            dma((sizes[1],)),
            dma((sizes[1],)),
        ],
        compiler_params=pltpu.CompilerParams(collective_id=1, has_side_effects=True),
        name="table_sum",
    )(table)


def padded(cells, sides, width):
    for axis, dim in sides:
        count = lax.axis_size(axis)
        ends = count - 1
        head = lax.slice_in_dim(cells, 0, width, axis=dim)
        tail = lax.slice_in_dim(cells, cells.shape[dim] - width, cells.shape[dim], axis=dim)
        cells = jnp.concatenate(
            [
                lax.ppermute(tail, axis, [(i, (i + 1) % count) for i in range(ends)]),
                cells,
                lax.ppermute(head, axis, [((i + 1) % count, i) for i in range(ends)]),
            ],
            axis=dim,
        )
    return cells


def angles(left, right, period):
    product = left[:, None] * right[None, :] % period
    return 2.0 * math.pi / period * product.astype(jnp.float32)


def on_device(spec_grad, transients, kernels, shifts, tiles):
    n_tm = lax.axis_size("tm")
    tm_index = lax.axis_index("tm")
    windows = spec_grad.shape[0]
    stretch = spec_grad.shape[2]
    total = N1 * N2
    rows_f2 = N2 // n_tm
    rows_f1 = N1 // n_tm
    local = spec_grad.reshape(windows, 2, rows_f2, N1)
    moved = lax.all_to_all(local, "tm", split_axis=3, concat_axis=2, tiled=True)
    freq_two = jnp.arange(N2, dtype=jnp.int32)
    freq_one = tm_index * rows_f1 + jnp.arange(rows_f1, dtype=jnp.int32)
    time_two = jnp.arange(N2, dtype=jnp.int32)
    phase_two = angles(freq_two, time_two, N2)
    cos_two = jnp.cos(phase_two)
    sin_two = jnp.sin(phase_two)
    real_in = moved[:, 0]
    imag_in = moved[:, 1]
    part_re = jnp.einsum("wfa,ft->wat", real_in, cos_two, precision=high) - jnp.einsum(
        "wfa,ft->wat", imag_in, sin_two, precision=high
    )
    part_im = jnp.einsum("wfa,ft->wat", real_in, sin_two, precision=high) + jnp.einsum(
        "wfa,ft->wat", imag_in, cos_two, precision=high
    )
    twiddle = angles(freq_one, time_two, total)
    cos_tw = jnp.cos(twiddle)[None]
    sin_tw = jnp.sin(twiddle)[None]
    turned = jnp.stack(
        [part_re * cos_tw - part_im * sin_tw, part_re * sin_tw + part_im * cos_tw], 1
    )
    columns = lax.all_to_all(turned, "tm", split_axis=3, concat_axis=2, tiled=True)
    all_one = jnp.arange(N1, dtype=jnp.int32)
    phase_one = angles(all_one, all_one, N1)
    rows_out = jnp.einsum("wfb,ft->wbt", columns[:, 0], jnp.cos(phase_one), precision=high)
    rows_out = rows_out - jnp.einsum(
        "wfb,ft->wbt", columns[:, 1], jnp.sin(phase_one), precision=high
    )
    rows_out = rows_out * total ** (-0.5)
    placed = lax.all_to_all(rows_out, "tm", split_axis=2, concat_axis=1, tiled=True)
    avg_grad = jnp.transpose(placed, (0, 2, 1)).reshape(windows, stretch)
    table, scan_grad = None, []
    cells = padded(avg_grad, (("tm", 1),), EDGE * LANES).reshape(windows, -1, LANES)
    cells = jnp.pad(cells, ((0, 0), (0, 14), (0, 0)))
    for w in range(windows):
        rows_w, table_w = scans_and_table(cells[w], transients[w], kernels, shifts[w], tiles[w])
        scan_grad.append(rows_w)
        table = table_w if table is None else table + table_w
    scan_grad = jnp.stack(scan_grad)
    sizes = (n_tm, lax.axis_size("scan"))
    if sizes[0] <= 8:
        table = sum_everywhere(table, sizes)
    else:
        table = lax.psum(table, ("tm", "scan"))
    return (scan_grad, table[:, :TILES].T)


def solution(mesh):
    placed = (P(None, None, "tm"), P(None, "scan", "tm"), P(), P(None, "scan"), P(None, "scan"))
    return jax.shard_map(
        on_device,
        mesh=mesh,
        in_specs=placed,
        out_specs=(P(None, "scan", "tm"), P()),
        check_vma=False,
    )
```

```python
import functools
import math

import jax
import jax.numpy as jnp
import numpy as np
from jax import lax
from jax.experimental import pallas as pl
from jax.experimental.pallas import tpu as pltpu
from jax.sharding import PartitionSpec as P

N1 = 1024
N2 = 1024
TILES = 16
TAPS = 16
KMAX = 512


highest = lax.Precision.HIGHEST
high = lax.Precision.HIGH
LANES = 128
EDGE = 8
MESH = pl.DeviceIdType.MESH


def halves(x):
    top = x.astype(jnp.bfloat16)
    return top, (x - top.astype(jnp.float32)).astype(jnp.bfloat16)


def fir_kernel(chunk, shifts_ref, tiles_ref, kernels_ref, g_ref, x_ref, out_ref, table_ref,
               gg, t_hi, t_lo, corr, xs, ys):
    step = pl.program_id(0)
    scans = x_ref.shape[0]
    rows = g_ref.shape[0] - 8

    def place(s):
        start = EDGE * LANES - TAPS // 2 + 1 - shifts_ref[s]
        return start // LANES, (start // (LANES // 2)) % 2, start % (LANES // 2)

    @pl.when(step == 0)
    def _():
        gg[0] = g_ref[:rows]
        lane = lax.broadcasted_iota(jnp.int32, (rows, LANES), 1)
        here = pltpu.roll(g_ref[:rows], LANES // 2, 1)
        nxt = pltpu.roll(g_ref[1 : rows + 1], LANES // 2, 1)
        gg[1] = jnp.where(lane < LANES // 2, here, nxt)
        row = lax.broadcasted_iota(jnp.int32, (2 * LANES, LANES), 0)
        col = lax.broadcasted_iota(jnp.int32, (2 * LANES, LANES), 1)

        def band(s, carry):
            _, _, o = place(s)
            tap = o + col + (TAPS - 1) - row
            value = jnp.zeros((2 * LANES, LANES), jnp.float32)
            for j in range(TAPS):
                value = jnp.where(tap == j, kernels_ref[tiles_ref[s], j], value)
            top, rest = halves(value)
            t_hi[s] = top
            t_lo[s] = rest
            corr[s] = jnp.zeros((LANES, 2 * LANES), jnp.float32)
            return carry

        lax.fori_loop(0, scans, band, 0)

    def split_in(r, carry):
        at = pl.ds(pl.multiple_of(r * LANES, LANES), LANES)
        xs[pl.ds(pl.multiple_of(r * scans, scans), scans), :] = x_ref[:, at].astype(jnp.float32)
        return carry

    lax.fori_loop(0, chunk, split_in, 0, unroll=8)

    for s in range(scans):
        q, c, _ = place(s)
        first = step * chunk + q
        window = jnp.concatenate(
            [gg[c, pl.ds(first, chunk), :], gg[c, pl.ds(first + 1, chunk), :]], axis=1
        )
        top, rest = halves(window)
        dot = functools.partial(jnp.dot, preferred_element_type=jnp.float32)
        ys[s * chunk : (s + 1) * chunk, :] = (
            dot(top, t_hi[s]) + (dot(top, t_lo[s]) + dot(rest, t_hi[s]))
        )
        x = xs[pl.ds(s, chunk, stride=scans), :].astype(jnp.bfloat16)
        down = functools.partial(
            lax.dot_general,
            dimension_numbers=(((0,), (0,)), ((), ())),
            preferred_element_type=jnp.float32,
        )
        corr[s] += down(x, top) + down(x, rest)

    def join_out(r, carry):
        at = pl.ds(pl.multiple_of(r * LANES, LANES), LANES)
        out_ref[:, at] = ys[pl.ds(r, scans, stride=chunk), :]
        return carry

    lax.fori_loop(0, chunk, join_out, 0, unroll=8)

    @pl.when(step == pl.num_programs(0) - 1)
    def _():
        apart = lax.broadcasted_iota(jnp.int32, (LANES, 2 * LANES), 1) - lax.broadcasted_iota(
            jnp.int32, (LANES, 2 * LANES), 0
        )
        tap = lax.broadcasted_iota(jnp.int32, (TAPS, LANES), 0)
        tile = lax.broadcasted_iota(jnp.int32, (TAPS, LANES), 1)

        def fold(s, total):
            _, _, o = place(s)
            values = corr[s]
            sums = [
                jnp.sum(jnp.where(apart == o + (TAPS - 1 - j), values, 0.0), axis=0, keepdims=True)
                for j in range(TAPS)
            ]
            column = jnp.sum(jnp.concatenate(sums, axis=0), axis=1, keepdims=True)
            return total + jnp.where(tile == tiles_ref[s], column, 0.0)

        table_ref[...] = lax.fori_loop(0, scans, fold, jnp.zeros((TAPS, LANES), jnp.float32))


def scans_and_table(padded_g, x, kernels, shifts, tiles):
    scans, stretch = x.shape
    rows = stretch // LANES
    chunk = min(256, rows)
    deep = padded_g.shape[0]
    smem = pl.BlockSpec(memory_space=pltpu.SMEM)
    return pl.pallas_call(
        functools.partial(fir_kernel, chunk),
        grid=(rows // chunk,),
        out_shape=[
            jax.ShapeDtypeStruct((scans, stretch), jnp.float32),
            jax.ShapeDtypeStruct((TAPS, LANES), jnp.float32),
        ],
        in_specs=[
            smem,
            smem,
            smem,
            pl.BlockSpec((deep, LANES), lambda i: (0, 0)),
            pl.BlockSpec((scans, chunk * LANES), lambda i: (0, i)),
        ],
        out_specs=[
            pl.BlockSpec((scans, chunk * LANES), lambda i: (0, i)),
            pl.BlockSpec((TAPS, LANES), lambda i: (0, 0)),
        ],
        scratch_shapes=[
            pltpu.VMEM((2, deep - 8, LANES), jnp.float32),
            pltpu.VMEM((scans, 2 * LANES, LANES), jnp.bfloat16),
            pltpu.VMEM((scans, 2 * LANES, LANES), jnp.bfloat16),
            pltpu.VMEM((scans, LANES, 2 * LANES), jnp.float32),
            pltpu.VMEM((scans * chunk, LANES), jnp.float32),
            pltpu.VMEM((scans * chunk, LANES), jnp.float32),
        ],
        compiler_params=pltpu.CompilerParams(vmem_limit_bytes=40 * 2**20),
        name="fir",
    )(shifts, tiles, kernels, padded_g, x)


def sum_kernel(sizes, in_ref, out_ref, first, second, send, recv, send2, recv2):
    here = [lax.axis_index("tm"), lax.axis_index("scan")]
    barrier = pltpu.get_barrier_semaphore()

    def peer(axis, k):
        other = list(here)
        other[axis] = lax.rem(here[axis] + k, sizes[axis])
        return tuple(other)

    for axis in range(2):
        for k in range(1, sizes[axis]):
            pl.semaphore_signal(barrier, inc=1, device_id=peer(axis, k), device_id_type=MESH)
    pl.semaphore_wait(barrier, sizes[0] + sizes[1] - 2)
    value = in_ref[...]
    for axis, slots, out_sem, in_sem in ((0, first, send, recv), (1, second, send2, recv2)):
        slots[here[axis]] = value
        copies = [
            pltpu.make_async_remote_copy(
                src_ref=slots.at[here[axis]],
                dst_ref=slots.at[here[axis]],
                send_sem=out_sem.at[k],
                recv_sem=in_sem.at[k],
                device_id=peer(axis, k),
                device_id_type=MESH,
            )
            for k in range(1, sizes[axis])
        ]
        for copy in copies:
            copy.start()
        for copy in copies:
            copy.wait()
        value = slots[0]
        for k in range(1, sizes[axis]):
            value = value + slots[k]
    out_ref[...] = value


def sum_everywhere(table, sizes):
    dma = pltpu.SemaphoreType.DMA
    vmem = pl.BlockSpec(memory_space=pltpu.VMEM)
    return pl.pallas_call(
        functools.partial(sum_kernel, sizes),
        out_shape=jax.ShapeDtypeStruct(table.shape, table.dtype),
        in_specs=[vmem],
        out_specs=vmem,
        scratch_shapes=[
            pltpu.VMEM((sizes[0],) + table.shape, table.dtype),
            pltpu.VMEM((sizes[1],) + table.shape, table.dtype),
            dma((sizes[0],)),
            dma((sizes[0],)),
            dma((sizes[1],)),
            dma((sizes[1],)),
        ],
        compiler_params=pltpu.CompilerParams(collective_id=1, has_side_effects=True),
        name="table_sum",
    )(table)


def padded(cells, sides, width):
    for axis, dim in sides:
        count = lax.axis_size(axis)
        ends = count - 1
        head = lax.slice_in_dim(cells, 0, width, axis=dim)
        tail = lax.slice_in_dim(cells, cells.shape[dim] - width, cells.shape[dim], axis=dim)
        cells = jnp.concatenate(
            [
                lax.ppermute(tail, axis, [(i, (i + 1) % count) for i in range(ends)]),
                cells,
                lax.ppermute(head, axis, [((i + 1) % count, i) for i in range(ends)]),
            ],
            axis=dim,
        )
    return cells


def angles(left, right, period):
    product = left[:, None] * right[None, :] % period
    return 2.0 * math.pi / period * product.astype(jnp.float32)


def two_terms(table):
    table = np.asarray(table, np.float32)
    top = table.astype(jnp.bfloat16)
    return top, (table - top.astype(np.float32)).astype(jnp.bfloat16)


@functools.lru_cache
def transform_tables(n_tm, n_scan):
    devices = n_tm * n_scan
    pairs = N1 // 2 // devices
    index = np.arange(N2)
    angle = 2.0 * np.pi / N2 * (index[:, None] * index[None, :] % N2)
    slots = np.arange(N1 // 2).reshape(devices, pairs)
    mirror = np.where(slots == 0, N1 // 2, N1 - slots)
    residues = np.concatenate([slots, mirror], axis=1)
    turn = 2.0 * np.pi / (N1 * N2) * (residues[:, :, None] * index)
    time = np.arange(N1).reshape(n_tm, n_scan, -1).transpose(1, 0, 2).reshape(-1)
    last = 2.0 * np.pi / N1 * (time[:, None, None] * slots[None] % N1)
    minus = np.where(slots[None] == 0, 1.0 - 2.0 * (time[:, None, None] % 2), -np.sin(last))
    final = np.concatenate([np.cos(last), minus], axis=2).reshape(n_scan, N1 // n_scan, N1)
    final = final * float(N1 * N2) ** -0.5
    return (
        *two_terms(np.cos(angle)),
        *two_terms(np.sin(angle)),
        np.cos(turn).astype(np.float32),
        np.sin(turn).astype(np.float32),
        *two_terms(final),
    )


def transform_kernel(n_tm, n_scan, spec_ref, cos_h, cos_l, sin_h, sin_l, turn_c, turn_s, fin_h, fin_l, out_ref,
                     vcos_h, vcos_l, vsin_h, vsin_l, vturn_c, vturn_s, vfin_h, vfin_l,
                     x_out, x_in, b_out, b_all, y_out, y_all, e_out, e_in, local_sem, send, recv):
    d, s = lax.axis_index("tm"), lax.axis_index("scan")
    mine = s * n_tm + d
    pairs = x_out.shape[1] // 2
    barrier = pltpu.get_barrier_semaphore()
    lines = [(lax.rem(d + k, n_tm), s) for k in range(1, n_tm)]
    columns = [(d, lax.rem(s + k, n_scan)) for k in range(1, n_scan)]
    for peer in lines + columns:
        pl.semaphore_signal(barrier, inc=1, device_id=peer, device_id_type=MESH)

    loads = [
        pltpu.make_async_copy(source, target, local_sem.at[i])
        for i, (source, target) in enumerate(
            (
                (cos_h, vcos_h),
                (cos_l, vcos_l),
                (sin_h, vsin_h),
                (sin_l, vsin_l),
                (turn_c.at[mine], vturn_c),
                (turn_s.at[mine], vturn_s),
                (fin_h.at[s], vfin_h),
                (fin_l.at[s], vfin_l),
            )
        )
    ]
    for load in loads:
        load.start()

    def remote(phase, k, source, target, peer):
        return pltpu.make_async_remote_copy(
            src_ref=source,
            dst_ref=target,
            send_sem=send.at[phase, k],
            recv_sem=recv.at[phase, k],
            device_id=peer,
            device_id_type=MESH,
        )

    def exchange(phase, blocks, target):
        copies = [
            remote(phase, k, blocks.at[peer[0]], target, peer) for k, peer in enumerate(lines)
        ]
        for copy in copies:
            copy.start()
        return copies

    def spread(phase, block):
        copies = [remote(phase, k, block, block, peer) for k, peer in enumerate(columns)]
        for copy in copies:
            copy.start()
        return copies

    def finish(copies):
        for copy in copies:
            copy.wait()

    dot = functools.partial(jnp.dot, preferred_element_type=jnp.float32)
    across = functools.partial(
        lax.dot_general,
        dimension_numbers=(((1,), (1,)), ((), ())),
        preferred_element_type=jnp.float32,
    )
    height = n_tm * 2 * pairs
    row = lax.broadcasted_iota(jnp.int32, (height, N1), 0)
    col = lax.broadcasted_iota(jnp.int32, (height, N1), 1)
    inner = row % (2 * pairs)
    slot = pairs * (s * n_tm + row // (2 * pairs)) + inner % pairs
    partner = jnp.where(slot == 0, N1 // 2, N1 - slot)
    pick = jnp.where(col == jnp.where(inner < pairs, slot, partner), 1.0, 0.0).astype(jnp.bfloat16)
    top, rest = halves(spec_ref[...])
    x_out[...] = (across(pick, top) + across(pick, rest)).reshape(x_out.shape)
    pl.semaphore_wait(barrier, len(lines) + len(columns))
    moving = exchange(0, x_out, x_in.at[d])
    x_in[d] = x_out[d]
    for load in loads:
        load.wait()
    finish(moving)

    real = jnp.concatenate([x_in[i, :, :LANES] for i in range(n_tm)], axis=1)
    imag = jnp.concatenate([x_in[i, :, LANES:] for i in range(n_tm)], axis=1)
    top, rest = halves(jnp.concatenate([real, imag], axis=0))
    both = jnp.concatenate([top, rest], axis=0)
    count = 4 * pairs

    def turned(high_table, low_table):
        big = dot(both, high_table[...])
        total = big[:count] + (big[count:] + dot(top, low_table[...]))
        return total[: 2 * pairs], total[2 * pairs :]

    re_cos, im_cos = turned(vcos_h, vcos_l)
    re_sin, im_sin = turned(vsin_h, vsin_l)
    part_re = re_cos - im_sin
    part_im = re_sin + im_cos
    a_re = vturn_c[...] * part_re - vturn_s[...] * part_im
    a_im = vturn_s[...] * part_re + vturn_c[...] * part_im
    alone = jnp.logical_and(lax.broadcasted_iota(jnp.int32, (pairs, N2), 0) == 0, mine == 0)
    b_re = jnp.where(alone, a_re[:pairs], a_re[:pairs] + a_re[pairs:])
    b_im = jnp.where(alone, a_re[pairs:], a_im[:pairs] - a_im[pairs:])
    for i in range(n_tm):
        b_out[i, :pairs] = b_re[:, i * LANES : (i + 1) * LANES]
        b_out[i, pairs:] = b_im[:, i * LANES : (i + 1) * LANES]
    moving = exchange(1, b_out, b_all.at[s, d])
    b_all[s, d] = b_out[d]
    finish(moving)
    finish(spread(2, b_all.at[s]))

    top, rest = halves(b_all[...].reshape(N1, LANES))
    rows_out = dot(vfin_h[...], top) + (dot(vfin_h[...], rest) + dot(vfin_l[...], top))
    y_out[...] = rows_out.reshape(y_out.shape)
    moving = exchange(3, y_out, y_all.at[s, d])
    y_all[s, d] = y_out[d]
    finish(moving)
    finish(spread(4, y_all.at[s]))

    deep = y_out.shape[1]
    for i in range(n_scan):
        for j in range(n_tm):
            out_ref[pl.ds(EDGE + i * deep * n_tm + j, deep, stride=n_tm), :] = y_all[i, j]
    stretch = n_scan * n_tm * deep
    e_out[0] = out_ref[EDGE : 2 * EDGE]
    e_out[1] = out_ref[stretch : stretch + EDGE]
    edges = [
        remote(5, 0, e_out.at[1], e_in.at[0], (lax.rem(d + 1, n_tm), s)),
        remote(5, 1, e_out.at[0], e_in.at[1], (lax.rem(d + n_tm - 1, n_tm), s)),
    ]
    for copy in edges:
        copy.start()
    finish(edges)
    out_ref[:EDGE] = jnp.where(d == 0, 0.0, e_in[0])
    out_ref[EDGE + stretch : 2 * EDGE + stretch] = jnp.where(d == n_tm - 1, 0.0, e_in[1])
    out_ref[2 * EDGE + stretch :] = jnp.zeros((8, LANES), jnp.float32)


def transform(spec, n_tm, n_scan):
    tables = [jnp.asarray(t) for t in transform_tables(n_tm, n_scan)]
    pairs = N1 // 2 // (n_tm * n_scan)
    part = N1 // n_tm // n_scan
    rows = N1 // n_tm * N2 // LANES
    dma = pltpu.SemaphoreType.DMA
    f32, bf16 = jnp.float32, jnp.bfloat16
    vmem = pl.BlockSpec(memory_space=pltpu.VMEM)
    return pl.pallas_call(
        functools.partial(transform_kernel, n_tm, n_scan),
        out_shape=jax.ShapeDtypeStruct((rows + 2 * EDGE + 8, LANES), f32),
        in_specs=[vmem] + [pl.BlockSpec(memory_space=pl.ANY)] * len(tables),
        out_specs=vmem,
        scratch_shapes=[
            pltpu.VMEM((N2, N2), bf16),
            pltpu.VMEM((N2, N2), bf16),
            pltpu.VMEM((N2, N2), bf16),
            pltpu.VMEM((N2, N2), bf16),
            pltpu.VMEM((2 * pairs, N2), f32),
            pltpu.VMEM((2 * pairs, N2), f32),
            pltpu.VMEM((N1 // n_scan, N1), bf16),
            pltpu.VMEM((N1 // n_scan, N1), bf16),
            pltpu.VMEM((n_tm, 2 * pairs, 2 * LANES), f32),
            pltpu.VMEM((n_tm, 2 * pairs, 2 * LANES), f32),
            pltpu.VMEM((n_tm, 2 * pairs, LANES), f32),
            pltpu.VMEM((n_scan, n_tm, 2 * pairs, LANES), f32),
            pltpu.VMEM((n_tm, part, LANES), f32),
            pltpu.VMEM((n_scan, n_tm, part, LANES), f32),
            pltpu.VMEM((2, EDGE, LANES), f32),
            pltpu.VMEM((2, EDGE, LANES), f32),
            dma((len(tables),)),
            dma((6, n_tm)),
            dma((6, n_tm)),
        ],
        compiler_params=pltpu.CompilerParams(
            collective_id=2, has_side_effects=True, vmem_limit_bytes=40 * 2**20
        ),
        name="transform",
    )(spec, *tables)


def general_transform(spec_grad):
    n_tm = lax.axis_size("tm")
    tm_index = lax.axis_index("tm")
    windows = spec_grad.shape[0]
    stretch = spec_grad.shape[2]
    total = N1 * N2
    rows_f2 = N2 // n_tm
    rows_f1 = N1 // n_tm
    local = spec_grad.reshape(windows, 2, rows_f2, N1)
    moved = lax.all_to_all(local, "tm", split_axis=3, concat_axis=2, tiled=True)
    freq_two = jnp.arange(N2, dtype=jnp.int32)
    freq_one = tm_index * rows_f1 + jnp.arange(rows_f1, dtype=jnp.int32)
    time_two = jnp.arange(N2, dtype=jnp.int32)
    phase_two = angles(freq_two, time_two, N2)
    cos_two = jnp.cos(phase_two)
    sin_two = jnp.sin(phase_two)
    real_in = moved[:, 0]
    imag_in = moved[:, 1]
    part_re = jnp.einsum("wfa,ft->wat", real_in, cos_two, precision=high) - jnp.einsum(
        "wfa,ft->wat", imag_in, sin_two, precision=high
    )
    part_im = jnp.einsum("wfa,ft->wat", real_in, sin_two, precision=high) + jnp.einsum(
        "wfa,ft->wat", imag_in, cos_two, precision=high
    )
    twiddle = angles(freq_one, time_two, total)
    cos_tw = jnp.cos(twiddle)[None]
    sin_tw = jnp.sin(twiddle)[None]
    turned = jnp.stack(
        [part_re * cos_tw - part_im * sin_tw, part_re * sin_tw + part_im * cos_tw], 1
    )
    columns = lax.all_to_all(turned, "tm", split_axis=3, concat_axis=2, tiled=True)
    all_one = jnp.arange(N1, dtype=jnp.int32)
    phase_one = angles(all_one, all_one, N1)
    rows_out = jnp.einsum("wfb,ft->wbt", columns[:, 0], jnp.cos(phase_one), precision=high)
    rows_out = rows_out - jnp.einsum(
        "wfb,ft->wbt", columns[:, 1], jnp.sin(phase_one), precision=high
    )
    rows_out = rows_out * total ** (-0.5)
    placed = lax.all_to_all(rows_out, "tm", split_axis=2, concat_axis=1, tiled=True)
    avg_grad = jnp.transpose(placed, (0, 2, 1)).reshape(windows, stretch)
    cells = padded(avg_grad, (("tm", 1),), EDGE * LANES).reshape(windows, -1, LANES)
    return jnp.pad(cells, ((0, 0), (0, 8), (0, 0)))


def on_device(spec_grad, transients, kernels, shifts, tiles):
    n_tm, n_scan = lax.axis_size("tm"), lax.axis_size("scan")
    windows = spec_grad.shape[0]
    if windows == 1 and N2 // n_tm == LANES and N1 // 2 % (8 * n_tm * n_scan) == 0:
        cells = transform(spec_grad.reshape(2 * LANES, N1), n_tm, n_scan)[None]
    else:
        cells = general_transform(spec_grad)
    table, scan_grad = None, []
    for w in range(windows):
        rows_w, table_w = scans_and_table(cells[w], transients[w], kernels, shifts[w], tiles[w])
        scan_grad.append(rows_w)
        table = table_w if table is None else table + table_w
    scan_grad = jnp.stack(scan_grad)
    sizes = (n_tm, n_scan)
    if sizes[0] <= 8:
        table = sum_everywhere(table, sizes)
    else:
        table = lax.psum(table, ("tm", "scan"))
    return (scan_grad, table[:, :TILES].T)


def solution(mesh):
    placed = (P(None, None, "tm"), P(None, "scan", "tm"), P(), P(None, "scan"), P(None, "scan"))
    return jax.shard_map(
        on_device,
        mesh=mesh,
        in_specs=placed,
        out_specs=(P(None, "scan", "tm"), P()),
        check_vma=False,
    )
```

```python
import functools
import math

import jax
import jax.numpy as jnp
import numpy as np
from jax import lax
from jax.experimental import pallas as pl
from jax.experimental.pallas import tpu as pltpu
from jax.sharding import PartitionSpec as P

N1 = 1024
N2 = 1024
TILES = 16
TAPS = 16
KMAX = 512


highest = lax.Precision.HIGHEST
high = lax.Precision.HIGH
LANES = 128
EDGE = 8
MESH = pl.DeviceIdType.MESH


def halves(x):
    top = x.astype(jnp.bfloat16)
    return top, (x - top.astype(jnp.float32)).astype(jnp.bfloat16)


def fir_kernel(chunk, shifts_ref, tiles_ref, kernels_ref, g_ref, x_ref, out_ref, table_ref,
               gg, t_hi, t_lo, corr, xs, ys):
    step = pl.program_id(0)
    scans = x_ref.shape[0]
    rows = g_ref.shape[0] - 8

    def place(s):
        start = EDGE * LANES - TAPS // 2 + 1 - shifts_ref[s]
        return start // LANES, (start // (LANES // 2)) % 2, start % (LANES // 2)

    @pl.when(step == 0)
    def _():
        gg[0] = g_ref[:rows]
        lane = lax.broadcasted_iota(jnp.int32, (rows, LANES), 1)
        here = pltpu.roll(g_ref[:rows], LANES // 2, 1)
        nxt = pltpu.roll(g_ref[1 : rows + 1], LANES // 2, 1)
        gg[1] = jnp.where(lane < LANES // 2, here, nxt)
        row = lax.broadcasted_iota(jnp.int32, (2 * LANES, LANES), 0)
        col = lax.broadcasted_iota(jnp.int32, (2 * LANES, LANES), 1)

        def band(s, carry):
            _, _, o = place(s)
            tap = o + col + (TAPS - 1) - row
            value = jnp.zeros((2 * LANES, LANES), jnp.float32)
            for j in range(TAPS):
                value = jnp.where(tap == j, kernels_ref[tiles_ref[s], j], value)
            top, rest = halves(value)
            t_hi[s] = top
            t_lo[s] = rest
            corr[s] = jnp.zeros((LANES, 2 * LANES), jnp.float32)
            return carry

        lax.fori_loop(0, scans, band, 0)

    def split_in(r, carry):
        at = pl.ds(pl.multiple_of(r * LANES, LANES), LANES)
        xs[pl.ds(pl.multiple_of(r * scans, scans), scans), :] = x_ref[:, at].astype(jnp.float32)
        return carry

    lax.fori_loop(0, chunk, split_in, 0, unroll=8)

    for s in range(scans):
        q, c, _ = place(s)
        first = step * chunk + q
        window = jnp.concatenate(
            [gg[c, pl.ds(first, chunk), :], gg[c, pl.ds(first + 1, chunk), :]], axis=1
        )
        top, rest = halves(window)
        dot = functools.partial(jnp.dot, preferred_element_type=jnp.float32)
        ys[s * chunk : (s + 1) * chunk, :] = (
            dot(top, t_hi[s]) + (dot(top, t_lo[s]) + dot(rest, t_hi[s]))
        )
        x = xs[pl.ds(s, chunk, stride=scans), :].astype(jnp.bfloat16)
        down = functools.partial(
            lax.dot_general,
            dimension_numbers=(((0,), (0,)), ((), ())),
            preferred_element_type=jnp.float32,
        )
        corr[s] += down(x, top) + down(x, rest)

    def join_out(r, carry):
        at = pl.ds(pl.multiple_of(r * LANES, LANES), LANES)
        out_ref[:, at] = ys[pl.ds(r, scans, stride=chunk), :]
        return carry

    lax.fori_loop(0, chunk, join_out, 0, unroll=8)

    @pl.when(step == pl.num_programs(0) - 1)
    def _():
        apart = lax.broadcasted_iota(jnp.int32, (LANES, 2 * LANES), 1) - lax.broadcasted_iota(
            jnp.int32, (LANES, 2 * LANES), 0
        )
        tap = lax.broadcasted_iota(jnp.int32, (TAPS, LANES), 0)
        tile = lax.broadcasted_iota(jnp.int32, (TAPS, LANES), 1)

        def fold(s, total):
            _, _, o = place(s)
            values = corr[s]
            sums = [
                jnp.sum(jnp.where(apart == o + (TAPS - 1 - j), values, 0.0), axis=0, keepdims=True)
                for j in range(TAPS)
            ]
            column = jnp.sum(jnp.concatenate(sums, axis=0), axis=1, keepdims=True)
            line = jnp.sum(jnp.where(tap == tile, column, 0.0), axis=0, keepdims=True)
            return total + jnp.where(tap == tiles_ref[s], line, 0.0)

        table_ref[...] = lax.fori_loop(0, scans, fold, jnp.zeros((TAPS, LANES), jnp.float32))


def scans_and_table(padded_g, x, kernels, shifts, tiles):
    scans, stretch = x.shape
    rows = stretch // LANES
    chunk = min(256, rows)
    deep = padded_g.shape[0]
    smem = pl.BlockSpec(memory_space=pltpu.SMEM)
    return pl.pallas_call(
        functools.partial(fir_kernel, chunk),
        grid=(rows // chunk,),
        out_shape=[
            jax.ShapeDtypeStruct((scans, stretch), jnp.float32),
            jax.ShapeDtypeStruct((TAPS, LANES), jnp.float32),
        ],
        in_specs=[
            smem,
            smem,
            smem,
            pl.BlockSpec((deep, LANES), lambda i: (0, 0)),
            pl.BlockSpec((scans, chunk * LANES), lambda i: (0, i)),
        ],
        out_specs=[
            pl.BlockSpec((scans, chunk * LANES), lambda i: (0, i)),
            pl.BlockSpec((TAPS, LANES), lambda i: (0, 0)),
        ],
        scratch_shapes=[
            pltpu.VMEM((2, deep - 8, LANES), jnp.float32),
            pltpu.VMEM((scans, 2 * LANES, LANES), jnp.bfloat16),
            pltpu.VMEM((scans, 2 * LANES, LANES), jnp.bfloat16),
            pltpu.VMEM((scans, LANES, 2 * LANES), jnp.float32),
            pltpu.VMEM((scans * chunk, LANES), jnp.float32),
            pltpu.VMEM((scans * chunk, LANES), jnp.float32),
        ],
        compiler_params=pltpu.CompilerParams(vmem_limit_bytes=40 * 2**20),
        name="fir",
    )(shifts, tiles, kernels, padded_g, x)


def sum_kernel(sizes, in_ref, out_ref, first, second, send, recv, send2, recv2):
    here = [lax.axis_index("tm"), lax.axis_index("scan")]
    barrier = pltpu.get_barrier_semaphore()

    def peer(axis, k):
        other = list(here)
        other[axis] = lax.rem(here[axis] + k, sizes[axis])
        return tuple(other)

    for axis in range(2):
        for k in range(1, sizes[axis]):
            pl.semaphore_signal(barrier, inc=1, device_id=peer(axis, k), device_id_type=MESH)
    pl.semaphore_wait(barrier, sizes[0] + sizes[1] - 2)
    value = in_ref[...]
    for axis, slots, out_sem, in_sem in ((0, first, send, recv), (1, second, send2, recv2)):
        slots[here[axis]] = value
        copies = [
            pltpu.make_async_remote_copy(
                src_ref=slots.at[here[axis]],
                dst_ref=slots.at[here[axis]],
                send_sem=out_sem.at[k],
                recv_sem=in_sem.at[k],
                device_id=peer(axis, k),
                device_id_type=MESH,
            )
            for k in range(1, sizes[axis])
        ]
        for copy in copies:
            copy.start()
        for copy in copies:
            copy.wait()
        value = slots[0]
        for k in range(1, sizes[axis]):
            value = value + slots[k]
    out_ref[...] = value[:, :TAPS]


def sum_everywhere(table, sizes):
    dma = pltpu.SemaphoreType.DMA
    vmem = pl.BlockSpec(memory_space=pltpu.VMEM)
    return pl.pallas_call(
        functools.partial(sum_kernel, sizes),
        out_shape=jax.ShapeDtypeStruct((TILES, TAPS), table.dtype),
        in_specs=[vmem],
        out_specs=vmem,
        scratch_shapes=[
            pltpu.VMEM((sizes[0],) + table.shape, table.dtype),
            pltpu.VMEM((sizes[1],) + table.shape, table.dtype),
            dma((sizes[0],)),
            dma((sizes[0],)),
            dma((sizes[1],)),
            dma((sizes[1],)),
        ],
        compiler_params=pltpu.CompilerParams(collective_id=1, has_side_effects=True),
        name="table_sum",
    )(table)


def padded(cells, sides, width):
    for axis, dim in sides:
        count = lax.axis_size(axis)
        ends = count - 1
        head = lax.slice_in_dim(cells, 0, width, axis=dim)
        tail = lax.slice_in_dim(cells, cells.shape[dim] - width, cells.shape[dim], axis=dim)
        cells = jnp.concatenate(
            [
                lax.ppermute(tail, axis, [(i, (i + 1) % count) for i in range(ends)]),
                cells,
                lax.ppermute(head, axis, [((i + 1) % count, i) for i in range(ends)]),
            ],
            axis=dim,
        )
    return cells


def angles(left, right, period):
    product = left[:, None] * right[None, :] % period
    return 2.0 * math.pi / period * product.astype(jnp.float32)


def two_terms(table):
    table = np.asarray(table, np.float32)
    top = table.astype(jnp.bfloat16)
    return top, (table - top.astype(np.float32)).astype(jnp.bfloat16)


@functools.lru_cache
def transform_tables(n_tm, n_scan):
    devices = n_tm * n_scan
    pairs = N1 // 2 // devices
    index = np.arange(N2)
    angle = 2.0 * np.pi / N2 * (index[:, None] * index[None, :] % N2)
    slots = np.arange(N1 // 2).reshape(devices, pairs)
    mirror = np.where(slots == 0, N1 // 2, N1 - slots)
    residues = np.concatenate([slots, mirror], axis=1)
    turn = 2.0 * np.pi / (N1 * N2) * (residues[:, :, None] * index)
    time = np.arange(N1).reshape(n_tm, n_scan, -1).transpose(1, 0, 2).reshape(-1)
    last = 2.0 * np.pi / N1 * (time[:, None, None] * slots[None] % N1)
    minus = np.where(slots[None] == 0, 1.0 - 2.0 * (time[:, None, None] % 2), -np.sin(last))
    final = np.concatenate([np.cos(last), minus], axis=2).reshape(n_scan, N1 // n_scan, N1)
    final = final * float(N1 * N2) ** -0.5
    return (
        *two_terms(np.cos(angle)),
        *two_terms(np.sin(angle)),
        np.cos(turn).astype(np.float32),
        np.sin(turn).astype(np.float32),
        *two_terms(final),
    )


def transform_kernel(n_tm, n_scan, spec_ref, cos_h, cos_l, sin_h, sin_l, turn_c, turn_s, fin_h, fin_l, out_ref,
                     vcos_h, vcos_l, vsin_h, vsin_l, vturn_c, vturn_s, vfin_h, vfin_l,
                     x_out, x_in, b_out, b_all, y_out, y_all, e_out, e_in, local_sem, send, recv,
                     pass_send, pass_recv):
    d, s = lax.axis_index("tm"), lax.axis_index("scan")
    mine = s * n_tm + d
    pairs = x_out.shape[1] // 2
    barrier = pltpu.get_barrier_semaphore()
    lines = [(lax.rem(d + k, n_tm), s) for k in range(1, n_tm)]
    columns = [(d, s + 1 - 2 * lax.rem(s, 2)), (d, lax.rem(s + 2, n_scan))]
    for peer in lines + columns:
        pl.semaphore_signal(barrier, inc=1, device_id=peer, device_id_type=MESH)

    loads = [
        pltpu.make_async_copy(source, target, local_sem.at[i])
        for i, (source, target) in enumerate(
            (
                (cos_h, vcos_h),
                (cos_l, vcos_l),
                (sin_h, vsin_h),
                (sin_l, vsin_l),
                (turn_c.at[mine], vturn_c),
                (turn_s.at[mine], vturn_s),
                (fin_h.at[s], vfin_h),
                (fin_l.at[s], vfin_l),
            )
        )
    ]
    for load in loads:
        load.start()

    def remote(phase, k, source, target, peer):
        return pltpu.make_async_remote_copy(
            src_ref=source,
            dst_ref=target,
            send_sem=send.at[phase, k],
            recv_sem=recv.at[phase, k],
            device_id=peer,
            device_id_type=MESH,
        )

    def exchange(phase, blocks, target):
        copies = [
            remote(phase, k, blocks.at[peer[0]], target, peer) for k, peer in enumerate(lines)
        ]
        for copy in copies:
            copy.start()
        return copies

    mate, across_x = s + 1 - 2 * lax.rem(s, 2), lax.rem(s + 2, n_scan)

    def share(phase, blocks, full):
        moving = exchange(phase, blocks, full.at[s, d])
        full[s, d] = blocks[d]
        owners = [lax.rem(d + n_tm - k, n_tm) for k in range(n_tm)]

        def step(kind, j, row, column):
            block = full.at[row, owners[j]]
            copy = pltpu.make_async_remote_copy(
                src_ref=block,
                dst_ref=block,
                send_sem=pass_send.at[phase - 1, kind, j],
                recv_sem=pass_recv.at[phase - 1, kind, j],
                device_id=(d, column),
                device_id_type=MESH,
            )
            copy.start()
            return copy

        far, near, relayed = [], [], []
        for j in range(n_tm):
            if j:
                moving[j - 1].wait_recv()
            far.append(step(0, j, s, across_x))
            near.append(step(1, j, s, mate))
        for j in range(n_tm):
            far[j].wait_recv()
            relayed.append(step(2, j, across_x, mate))
        for copy in near + relayed:
            copy.wait_recv()
        for copy in moving + far + near + relayed:
            copy.wait_send()

    def finish(copies):
        for copy in copies:
            copy.wait()

    dot = functools.partial(jnp.dot, preferred_element_type=jnp.float32)
    across = functools.partial(
        lax.dot_general,
        dimension_numbers=(((1,), (1,)), ((), ())),
        preferred_element_type=jnp.float32,
    )
    height = n_tm * 2 * pairs
    row = lax.broadcasted_iota(jnp.int32, (height, N1), 0)
    col = lax.broadcasted_iota(jnp.int32, (height, N1), 1)
    inner = row % (2 * pairs)
    slot = pairs * (s * n_tm + row // (2 * pairs)) + inner % pairs
    partner = jnp.where(slot == 0, N1 // 2, N1 - slot)
    pick = jnp.where(col == jnp.where(inner < pairs, slot, partner), 1.0, 0.0).astype(jnp.bfloat16)
    top, rest = halves(spec_ref[...])
    x_out[...] = (across(pick, top) + across(pick, rest)).reshape(x_out.shape)
    pl.semaphore_wait(barrier, len(lines) + len(columns))
    moving = exchange(0, x_out, x_in.at[d])
    x_in[d] = x_out[d]
    for load in loads:
        load.wait()
    finish(moving)

    real = jnp.concatenate([x_in[i, :, :LANES] for i in range(n_tm)], axis=1)
    imag = jnp.concatenate([x_in[i, :, LANES:] for i in range(n_tm)], axis=1)
    top, rest = halves(jnp.concatenate([real, imag], axis=0))
    both = jnp.concatenate([top, rest], axis=0)
    count = 4 * pairs

    def turned(high_table, low_table):
        big = dot(both, high_table[...])
        total = big[:count] + (big[count:] + dot(top, low_table[...]))
        return total[: 2 * pairs], total[2 * pairs :]

    re_cos, im_cos = turned(vcos_h, vcos_l)
    re_sin, im_sin = turned(vsin_h, vsin_l)
    part_re = re_cos - im_sin
    part_im = re_sin + im_cos
    a_re = vturn_c[...] * part_re - vturn_s[...] * part_im
    a_im = vturn_s[...] * part_re + vturn_c[...] * part_im
    alone = jnp.logical_and(lax.broadcasted_iota(jnp.int32, (pairs, N2), 0) == 0, mine == 0)
    b_re = jnp.where(alone, a_re[:pairs], a_re[:pairs] + a_re[pairs:])
    b_im = jnp.where(alone, a_re[pairs:], a_im[:pairs] - a_im[pairs:])
    for i in range(n_tm):
        b_out[i, :pairs] = b_re[:, i * LANES : (i + 1) * LANES]
        b_out[i, pairs:] = b_im[:, i * LANES : (i + 1) * LANES]
    share(1, b_out, b_all)

    top, rest = halves(b_all[...].reshape(N1, LANES))
    rows_out = dot(vfin_h[...], top) + (dot(vfin_h[...], rest) + dot(vfin_l[...], top))
    y_out[...] = rows_out.reshape(y_out.shape)
    share(2, y_out, y_all)

    deep = y_out.shape[1]
    for i in range(n_scan):
        for j in range(n_tm):
            out_ref[pl.ds(EDGE + i * deep * n_tm + j, deep, stride=n_tm), :] = y_all[i, j]
    stretch = n_scan * n_tm * deep
    e_out[0] = out_ref[EDGE : 2 * EDGE]
    e_out[1] = out_ref[stretch : stretch + EDGE]
    edges = [
        remote(3, 0, e_out.at[1], e_in.at[0], (lax.rem(d + 1, n_tm), s)),
        remote(3, 1, e_out.at[0], e_in.at[1], (lax.rem(d + n_tm - 1, n_tm), s)),
    ]
    for copy in edges:
        copy.start()
    finish(edges)
    out_ref[:EDGE] = jnp.where(d == 0, 0.0, e_in[0])
    out_ref[EDGE + stretch : 2 * EDGE + stretch] = jnp.where(d == n_tm - 1, 0.0, e_in[1])
    out_ref[2 * EDGE + stretch :] = jnp.zeros((8, LANES), jnp.float32)


def transform(spec, n_tm, n_scan):
    tables = [jnp.asarray(t) for t in transform_tables(n_tm, n_scan)]
    pairs = N1 // 2 // (n_tm * n_scan)
    part = N1 // n_tm // n_scan
    rows = N1 // n_tm * N2 // LANES
    dma = pltpu.SemaphoreType.DMA
    f32, bf16 = jnp.float32, jnp.bfloat16
    vmem = pl.BlockSpec(memory_space=pltpu.VMEM)
    return pl.pallas_call(
        functools.partial(transform_kernel, n_tm, n_scan),
        out_shape=jax.ShapeDtypeStruct((rows + 2 * EDGE + 8, LANES), f32),
        in_specs=[vmem] + [pl.BlockSpec(memory_space=pl.ANY)] * len(tables),
        out_specs=vmem,
        scratch_shapes=[
            pltpu.VMEM((N2, N2), bf16),
            pltpu.VMEM((N2, N2), bf16),
            pltpu.VMEM((N2, N2), bf16),
            pltpu.VMEM((N2, N2), bf16),
            pltpu.VMEM((2 * pairs, N2), f32),
            pltpu.VMEM((2 * pairs, N2), f32),
            pltpu.VMEM((N1 // n_scan, N1), bf16),
            pltpu.VMEM((N1 // n_scan, N1), bf16),
            pltpu.VMEM((n_tm, 2 * pairs, 2 * LANES), f32),
            pltpu.VMEM((n_tm, 2 * pairs, 2 * LANES), f32),
            pltpu.VMEM((n_tm, 2 * pairs, LANES), f32),
            pltpu.VMEM((n_scan, n_tm, 2 * pairs, LANES), f32),
            pltpu.VMEM((n_tm, part, LANES), f32),
            pltpu.VMEM((n_scan, n_tm, part, LANES), f32),
            pltpu.VMEM((2, EDGE, LANES), f32),
            pltpu.VMEM((2, EDGE, LANES), f32),
            dma((len(tables),)),
            dma((4, n_tm)),
            dma((4, n_tm)),
            dma((2, 3, n_tm)),
            dma((2, 3, n_tm)),
        ],
        compiler_params=pltpu.CompilerParams(
            collective_id=2, has_side_effects=True, vmem_limit_bytes=58 * 2**20
        ),
        name="transform",
    )(spec, *tables)


def general_transform(spec_grad):
    n_tm = lax.axis_size("tm")
    tm_index = lax.axis_index("tm")
    windows = spec_grad.shape[0]
    stretch = spec_grad.shape[2]
    total = N1 * N2
    rows_f2 = N2 // n_tm
    rows_f1 = N1 // n_tm
    local = spec_grad.reshape(windows, 2, rows_f2, N1)
    moved = lax.all_to_all(local, "tm", split_axis=3, concat_axis=2, tiled=True)
    freq_two = jnp.arange(N2, dtype=jnp.int32)
    freq_one = tm_index * rows_f1 + jnp.arange(rows_f1, dtype=jnp.int32)
    time_two = jnp.arange(N2, dtype=jnp.int32)
    phase_two = angles(freq_two, time_two, N2)
    cos_two = jnp.cos(phase_two)
    sin_two = jnp.sin(phase_two)
    real_in = moved[:, 0]
    imag_in = moved[:, 1]
    part_re = jnp.einsum("wfa,ft->wat", real_in, cos_two, precision=high) - jnp.einsum(
        "wfa,ft->wat", imag_in, sin_two, precision=high
    )
    part_im = jnp.einsum("wfa,ft->wat", real_in, sin_two, precision=high) + jnp.einsum(
        "wfa,ft->wat", imag_in, cos_two, precision=high
    )
    twiddle = angles(freq_one, time_two, total)
    cos_tw = jnp.cos(twiddle)[None]
    sin_tw = jnp.sin(twiddle)[None]
    turned = jnp.stack(
        [part_re * cos_tw - part_im * sin_tw, part_re * sin_tw + part_im * cos_tw], 1
    )
    columns = lax.all_to_all(turned, "tm", split_axis=3, concat_axis=2, tiled=True)
    all_one = jnp.arange(N1, dtype=jnp.int32)
    phase_one = angles(all_one, all_one, N1)
    rows_out = jnp.einsum("wfb,ft->wbt", columns[:, 0], jnp.cos(phase_one), precision=high)
    rows_out = rows_out - jnp.einsum(
        "wfb,ft->wbt", columns[:, 1], jnp.sin(phase_one), precision=high
    )
    rows_out = rows_out * total ** (-0.5)
    placed = lax.all_to_all(rows_out, "tm", split_axis=2, concat_axis=1, tiled=True)
    avg_grad = jnp.transpose(placed, (0, 2, 1)).reshape(windows, stretch)
    cells = padded(avg_grad, (("tm", 1),), EDGE * LANES).reshape(windows, -1, LANES)
    return jnp.pad(cells, ((0, 0), (0, 8), (0, 0)))


def on_device(spec_grad, transients, kernels, shifts, tiles):
    n_tm, n_scan = lax.axis_size("tm"), lax.axis_size("scan")
    windows = spec_grad.shape[0]
    if windows == 1 and n_scan == 4 and N2 // n_tm == LANES and N1 // 2 % (8 * n_tm * n_scan) == 0:
        cells = transform(spec_grad.reshape(2 * LANES, N1), n_tm, n_scan)[None]
    else:
        cells = general_transform(spec_grad)
    table, scan_grad = None, []
    for w in range(windows):
        rows_w, table_w = scans_and_table(cells[w], transients[w], kernels, shifts[w], tiles[w])
        scan_grad.append(rows_w)
        table = table_w if table is None else table + table_w
    scan_grad = jnp.stack(scan_grad)
    sizes = (n_tm, n_scan)
    if sizes[0] <= 8:
        table = sum_everywhere(table, sizes)
    else:
        table = lax.psum(table[:, :TAPS], ("tm", "scan"))
    return (scan_grad, table)


def solution(mesh):
    placed = (P(None, None, "tm"), P(None, "scan", "tm"), P(), P(None, "scan"), P(None, "scan"))
    return jax.shard_map(
        on_device,
        mesh=mesh,
        in_specs=placed,
        out_specs=(P(None, "scan", "tm"), P()),
        check_vma=False,
    )
```

```python
import functools
import math

import jax
import jax.numpy as jnp
import numpy as np
from jax import lax
from jax.experimental import pallas as pl
from jax.experimental.pallas import tpu as pltpu
from jax.sharding import PartitionSpec as P

N1 = 1024
N2 = 1024
TILES = 16
TAPS = 16
KMAX = 512


highest = lax.Precision.HIGHEST
high = lax.Precision.HIGH
LANES = 128
EDGE = 8
MESH = pl.DeviceIdType.MESH


def halves(x):
    top = x.astype(jnp.bfloat16)
    return top, (x - top.astype(jnp.float32)).astype(jnp.bfloat16)


def fir_kernel(chunk, shifts_ref, tiles_ref, kernels_ref, g_ref, x_ref, out_ref, table_ref,
               gg, t_hi, t_lo, corr, xs, ys):
    step = pl.program_id(0)
    scans = x_ref.shape[0]
    rows = g_ref.shape[0] - 8

    def place(s):
        start = EDGE * LANES - TAPS // 2 + 1 - shifts_ref[s]
        return start // LANES, (start // (LANES // 2)) % 2, start % (LANES // 2)

    @pl.when(step == 0)
    def _():
        gg[0] = g_ref[:rows]
        lane = lax.broadcasted_iota(jnp.int32, (rows, LANES), 1)
        here = pltpu.roll(g_ref[:rows], LANES // 2, 1)
        nxt = pltpu.roll(g_ref[1 : rows + 1], LANES // 2, 1)
        gg[1] = jnp.where(lane < LANES // 2, here, nxt)
        row = lax.broadcasted_iota(jnp.int32, (2 * LANES, LANES), 0)
        col = lax.broadcasted_iota(jnp.int32, (2 * LANES, LANES), 1)

        def band(s, carry):
            _, _, o = place(s)
            tap = o + col + (TAPS - 1) - row
            value = jnp.zeros((2 * LANES, LANES), jnp.float32)
            for j in range(TAPS):
                value = jnp.where(tap == j, kernels_ref[tiles_ref[s], j], value)
            top, rest = halves(value)
            t_hi[s] = top
            t_lo[s] = rest
            corr[s] = jnp.zeros((LANES, 2 * LANES), jnp.float32)
            return carry

        lax.fori_loop(0, scans, band, 0)

    def split_in(r, carry):
        at = pl.ds(pl.multiple_of(r * LANES, LANES), LANES)
        xs[pl.ds(pl.multiple_of(r * scans, scans), scans), :] = x_ref[:, at].astype(jnp.float32)
        return carry

    lax.fori_loop(0, chunk, split_in, 0, unroll=32)

    for s in range(scans):
        q, c, _ = place(s)
        first = step * chunk + q
        window = jnp.concatenate(
            [gg[c, pl.ds(first, chunk), :], gg[c, pl.ds(first + 1, chunk), :]], axis=1
        )
        top, rest = halves(window)
        dot = functools.partial(jnp.dot, preferred_element_type=jnp.float32)
        ys[s * chunk : (s + 1) * chunk, :] = (
            dot(top, t_hi[s]) + (dot(top, t_lo[s]) + dot(rest, t_hi[s]))
        )
        x = xs[pl.ds(s, chunk, stride=scans), :].astype(jnp.bfloat16)
        down = functools.partial(
            lax.dot_general,
            dimension_numbers=(((0,), (0,)), ((), ())),
            preferred_element_type=jnp.float32,
        )
        corr[s] += down(x, top) + down(x, rest)

    def join_out(r, carry):
        at = pl.ds(pl.multiple_of(r * LANES, LANES), LANES)
        out_ref[:, at] = ys[pl.ds(r, scans, stride=chunk), :]
        return carry

    lax.fori_loop(0, chunk, join_out, 0, unroll=32)

    @pl.when(step == pl.num_programs(0) - 1)
    def _():
        apart = lax.broadcasted_iota(jnp.int32, (LANES, 2 * LANES), 1) - lax.broadcasted_iota(
            jnp.int32, (LANES, 2 * LANES), 0
        )
        tap = lax.broadcasted_iota(jnp.int32, (TAPS, LANES), 0)
        tile = lax.broadcasted_iota(jnp.int32, (TAPS, LANES), 1)

        def fold(s, total):
            _, _, o = place(s)
            values = corr[s]
            sums = [
                jnp.sum(jnp.where(apart == o + (TAPS - 1 - j), values, 0.0), axis=0, keepdims=True)
                for j in range(TAPS)
            ]
            column = jnp.sum(jnp.concatenate(sums, axis=0), axis=1, keepdims=True)
            line = jnp.sum(jnp.where(tap == tile, column, 0.0), axis=0, keepdims=True)
            return total + jnp.where(tap == tiles_ref[s], line, 0.0)

        table_ref[...] = lax.fori_loop(0, scans, fold, jnp.zeros((TAPS, LANES), jnp.float32))


def scans_and_table(padded_g, x, kernels, shifts, tiles):
    scans, stretch = x.shape
    rows = stretch // LANES
    chunk = min(256, rows)
    deep = padded_g.shape[0]
    smem = pl.BlockSpec(memory_space=pltpu.SMEM)
    return pl.pallas_call(
        functools.partial(fir_kernel, chunk),
        grid=(rows // chunk,),
        out_shape=[
            jax.ShapeDtypeStruct((scans, stretch), jnp.float32),
            jax.ShapeDtypeStruct((TAPS, LANES), jnp.float32),
        ],
        in_specs=[
            smem,
            smem,
            smem,
            pl.BlockSpec((deep, LANES), lambda i: (0, 0)),
            pl.BlockSpec((scans, chunk * LANES), lambda i: (0, i)),
        ],
        out_specs=[
            pl.BlockSpec((scans, chunk * LANES), lambda i: (0, i)),
            pl.BlockSpec((TAPS, LANES), lambda i: (0, 0)),
        ],
        scratch_shapes=[
            pltpu.VMEM((2, deep - 8, LANES), jnp.float32),
            pltpu.VMEM((scans, 2 * LANES, LANES), jnp.bfloat16),
            pltpu.VMEM((scans, 2 * LANES, LANES), jnp.bfloat16),
            pltpu.VMEM((scans, LANES, 2 * LANES), jnp.float32),
            pltpu.VMEM((scans * chunk, LANES), jnp.float32),
            pltpu.VMEM((scans * chunk, LANES), jnp.float32),
        ],
        compiler_params=pltpu.CompilerParams(vmem_limit_bytes=40 * 2**20),
        name="fir",
    )(shifts, tiles, kernels, padded_g, x)


def sum_kernel(sizes, in_ref, out_ref, slots, send, recv):
    d, s = lax.axis_index("tm"), lax.axis_index("scan")
    barrier = pltpu.get_barrier_semaphore()
    steps = [(i, j) for i in range(sizes[0]) for j in range(sizes[1])]
    peers = [(lax.rem(d + i, sizes[0]), lax.rem(s + j, sizes[1])) for i, j in steps[1:]]
    for peer in peers:
        pl.semaphore_signal(barrier, inc=1, device_id=peer, device_id_type=MESH)
    slots[d, s] = in_ref[...]
    pl.semaphore_wait(barrier, len(peers))
    copies = [
        pltpu.make_async_remote_copy(
            src_ref=slots.at[d, s],
            dst_ref=slots.at[d, s],
            send_sem=send.at[k],
            recv_sem=recv.at[k],
            device_id=peer,
            device_id_type=MESH,
        )
        for k, peer in enumerate(peers)
    ]
    for copy in copies:
        copy.start()
    for copy in copies:
        copy.wait()
    value = slots[0, 0]
    for i, j in steps[1:]:
        value = value + slots[i, j]
    out_ref[...] = value[:, :TAPS]


def sum_everywhere(table, sizes):
    dma = pltpu.SemaphoreType.DMA
    vmem = pl.BlockSpec(memory_space=pltpu.VMEM)
    return pl.pallas_call(
        functools.partial(sum_kernel, sizes),
        out_shape=jax.ShapeDtypeStruct((TILES, TAPS), table.dtype),
        in_specs=[vmem],
        out_specs=vmem,
        scratch_shapes=[
            pltpu.VMEM(sizes + table.shape, table.dtype),
            dma((sizes[0] * sizes[1],)),
            dma((sizes[0] * sizes[1],)),
        ],
        compiler_params=pltpu.CompilerParams(collective_id=1, has_side_effects=True),
        name="table_sum",
    )(table)


def padded(cells, sides, width):
    for axis, dim in sides:
        count = lax.axis_size(axis)
        ends = count - 1
        head = lax.slice_in_dim(cells, 0, width, axis=dim)
        tail = lax.slice_in_dim(cells, cells.shape[dim] - width, cells.shape[dim], axis=dim)
        cells = jnp.concatenate(
            [
                lax.ppermute(tail, axis, [(i, (i + 1) % count) for i in range(ends)]),
                cells,
                lax.ppermute(head, axis, [((i + 1) % count, i) for i in range(ends)]),
            ],
            axis=dim,
        )
    return cells


def angles(left, right, period):
    product = left[:, None] * right[None, :] % period
    return 2.0 * math.pi / period * product.astype(jnp.float32)


def two_terms(table):
    table = np.asarray(table, np.float32)
    top = table.astype(jnp.bfloat16)
    return top, (table - top.astype(np.float32)).astype(jnp.bfloat16)


@functools.lru_cache
def transform_tables(n_tm, n_scan):
    devices = n_tm * n_scan
    pairs = N1 // 2 // devices
    index = np.arange(N2)
    angle = 2.0 * np.pi / N2 * (index[:, None] * index[None, :] % N2)
    slots = np.arange(N1 // 2).reshape(devices, pairs)
    mirror = np.where(slots == 0, N1 // 2, N1 - slots)
    residues = np.concatenate([slots, mirror], axis=1)
    turn = 2.0 * np.pi / (N1 * N2) * (residues[:, :, None] * index)
    time = np.arange(N1).reshape(n_tm, n_scan, -1).transpose(1, 0, 2).reshape(-1)
    last = 2.0 * np.pi / N1 * (time[:, None, None] * slots[None] % N1)
    minus = np.where(slots[None] == 0, 1.0 - 2.0 * (time[:, None, None] % 2), -np.sin(last))
    final = np.concatenate([np.cos(last), minus], axis=2).reshape(n_scan, N1 // n_scan, N1)
    final = final * float(N1 * N2) ** -0.5
    return (
        *two_terms(np.cos(angle)),
        *two_terms(np.sin(angle)),
        np.cos(turn).astype(np.float32),
        np.sin(turn).astype(np.float32),
        *two_terms(final),
    )


def transform_kernel(n_tm, n_scan, spec_ref, cos_h, cos_l, sin_h, sin_l, turn_c, turn_s, fin_h, fin_l, out_ref,
                     vcos_h, vcos_l, vsin_h, vsin_l, vturn_c, vturn_s, vfin_h, vfin_l,
                     x_out, x_in, b_out, b_all, y_out, y_all, e_out, e_in, local_sem, send, recv,
                     pass_send, pass_recv):
    d, s = lax.axis_index("tm"), lax.axis_index("scan")
    mine = s * n_tm + d
    pairs = x_out.shape[1] // 2
    barrier = pltpu.get_barrier_semaphore()
    lines = [(lax.rem(d + k, n_tm), s) for k in range(1, n_tm)]
    columns = [(d, s + 1 - 2 * lax.rem(s, 2)), (d, lax.rem(s + 2, n_scan))]
    for peer in lines + columns:
        pl.semaphore_signal(barrier, inc=1, device_id=peer, device_id_type=MESH)

    loads = [
        pltpu.make_async_copy(source, target, local_sem.at[i])
        for i, (source, target) in enumerate(
            (
                (cos_h, vcos_h),
                (cos_l, vcos_l),
                (sin_h, vsin_h),
                (sin_l, vsin_l),
                (turn_c.at[mine], vturn_c),
                (turn_s.at[mine], vturn_s),
                (fin_h.at[s], vfin_h),
                (fin_l.at[s], vfin_l),
            )
        )
    ]
    for load in loads:
        load.start()

    def remote(phase, k, source, target, peer):
        return pltpu.make_async_remote_copy(
            src_ref=source,
            dst_ref=target,
            send_sem=send.at[phase, k],
            recv_sem=recv.at[phase, k],
            device_id=peer,
            device_id_type=MESH,
        )

    def exchange(phase, blocks, target):
        copies = [
            remote(phase, k, blocks.at[peer[0]], target, peer) for k, peer in enumerate(lines)
        ]
        for copy in copies:
            copy.start()
        return copies

    mate, across_x = s + 1 - 2 * lax.rem(s, 2), lax.rem(s + 2, n_scan)

    def share(phase, blocks, full):
        moving = exchange(phase, blocks, full.at[s, d])
        full[s, d] = blocks[d]
        owners = [lax.rem(d + n_tm - k, n_tm) for k in range(n_tm)]

        def step(kind, j, row, column):
            block = full.at[row, owners[j]]
            copy = pltpu.make_async_remote_copy(
                src_ref=block,
                dst_ref=block,
                send_sem=pass_send.at[phase - 1, kind, j],
                recv_sem=pass_recv.at[phase - 1, kind, j],
                device_id=(d, column),
                device_id_type=MESH,
            )
            copy.start()
            return copy

        far, near, relayed = [], [], []
        for j in range(n_tm):
            if j:
                moving[j - 1].wait_recv()
            far.append(step(0, j, s, across_x))
            near.append(step(1, j, s, mate))
        for j in range(n_tm):
            far[j].wait_recv()
            relayed.append(step(2, j, across_x, mate))
        for copy in near + relayed:
            copy.wait_recv()
        for copy in moving + far + near + relayed:
            copy.wait_send()

    def finish(copies):
        for copy in copies:
            copy.wait()

    dot = functools.partial(jnp.dot, preferred_element_type=jnp.float32)
    across = functools.partial(
        lax.dot_general,
        dimension_numbers=(((1,), (1,)), ((), ())),
        preferred_element_type=jnp.float32,
    )
    height = n_tm * 2 * pairs
    row = lax.broadcasted_iota(jnp.int32, (height, N1), 0)
    col = lax.broadcasted_iota(jnp.int32, (height, N1), 1)
    inner = row % (2 * pairs)
    slot = pairs * (s * n_tm + row // (2 * pairs)) + inner % pairs
    partner = jnp.where(slot == 0, N1 // 2, N1 - slot)
    pick = jnp.where(col == jnp.where(inner < pairs, slot, partner), 1.0, 0.0).astype(jnp.bfloat16)
    top, rest = halves(spec_ref[...])
    x_out[...] = (across(pick, top) + across(pick, rest)).reshape(x_out.shape)
    pl.semaphore_wait(barrier, len(lines) + len(columns))
    moving = exchange(0, x_out, x_in.at[d])
    x_in[d] = x_out[d]
    for load in loads:
        load.wait()
    finish(moving)

    real = jnp.concatenate([x_in[i, :, :LANES] for i in range(n_tm)], axis=1)
    imag = jnp.concatenate([x_in[i, :, LANES:] for i in range(n_tm)], axis=1)
    top, rest = halves(jnp.concatenate([real, imag], axis=0))
    both = jnp.concatenate([top, rest], axis=0)
    count = 4 * pairs

    def turned(high_table, low_table):
        big = dot(both, high_table[...])
        total = big[:count] + (big[count:] + dot(top, low_table[...]))
        return total[: 2 * pairs], total[2 * pairs :]

    re_cos, im_cos = turned(vcos_h, vcos_l)
    re_sin, im_sin = turned(vsin_h, vsin_l)
    part_re = re_cos - im_sin
    part_im = re_sin + im_cos
    a_re = vturn_c[...] * part_re - vturn_s[...] * part_im
    a_im = vturn_s[...] * part_re + vturn_c[...] * part_im
    alone = jnp.logical_and(lax.broadcasted_iota(jnp.int32, (pairs, N2), 0) == 0, mine == 0)
    b_re = jnp.where(alone, a_re[:pairs], a_re[:pairs] + a_re[pairs:])
    b_im = jnp.where(alone, a_re[pairs:], a_im[:pairs] - a_im[pairs:])
    for i in range(n_tm):
        b_out[i, :pairs] = b_re[:, i * LANES : (i + 1) * LANES]
        b_out[i, pairs:] = b_im[:, i * LANES : (i + 1) * LANES]
    share(1, b_out, b_all)

    top, rest = halves(b_all[...].reshape(N1, LANES))
    rows_out = dot(vfin_h[...], top) + (dot(vfin_h[...], rest) + dot(vfin_l[...], top))
    y_out[...] = rows_out.reshape(y_out.shape)
    share(2, y_out, y_all)

    deep = y_out.shape[1]
    for i in range(n_scan):
        for j in range(n_tm):
            out_ref[pl.ds(EDGE + i * deep * n_tm + j, deep, stride=n_tm), :] = y_all[i, j]
    stretch = n_scan * n_tm * deep
    e_out[0] = out_ref[EDGE : 2 * EDGE]
    e_out[1] = out_ref[stretch : stretch + EDGE]
    edges = [
        remote(3, 0, e_out.at[1], e_in.at[0], (lax.rem(d + 1, n_tm), s)),
        remote(3, 1, e_out.at[0], e_in.at[1], (lax.rem(d + n_tm - 1, n_tm), s)),
    ]
    for copy in edges:
        copy.start()
    finish(edges)
    out_ref[:EDGE] = jnp.where(d == 0, 0.0, e_in[0])
    out_ref[EDGE + stretch : 2 * EDGE + stretch] = jnp.where(d == n_tm - 1, 0.0, e_in[1])
    out_ref[2 * EDGE + stretch :] = jnp.zeros((8, LANES), jnp.float32)


def transform(spec, n_tm, n_scan):
    tables = [jnp.asarray(t) for t in transform_tables(n_tm, n_scan)]
    pairs = N1 // 2 // (n_tm * n_scan)
    part = N1 // n_tm // n_scan
    rows = N1 // n_tm * N2 // LANES
    dma = pltpu.SemaphoreType.DMA
    f32, bf16 = jnp.float32, jnp.bfloat16
    vmem = pl.BlockSpec(memory_space=pltpu.VMEM)
    return pl.pallas_call(
        functools.partial(transform_kernel, n_tm, n_scan),
        out_shape=jax.ShapeDtypeStruct((rows + 2 * EDGE + 8, LANES), f32),
        in_specs=[vmem] + [pl.BlockSpec(memory_space=pl.ANY)] * len(tables),
        out_specs=vmem,
        scratch_shapes=[
            pltpu.VMEM((N2, N2), bf16),
            pltpu.VMEM((N2, N2), bf16),
            pltpu.VMEM((N2, N2), bf16),
            pltpu.VMEM((N2, N2), bf16),
            pltpu.VMEM((2 * pairs, N2), f32),
            pltpu.VMEM((2 * pairs, N2), f32),
            pltpu.VMEM((N1 // n_scan, N1), bf16),
            pltpu.VMEM((N1 // n_scan, N1), bf16),
            pltpu.VMEM((n_tm, 2 * pairs, 2 * LANES), f32),
            pltpu.VMEM((n_tm, 2 * pairs, 2 * LANES), f32),
            pltpu.VMEM((n_tm, 2 * pairs, LANES), f32),
            pltpu.VMEM((n_scan, n_tm, 2 * pairs, LANES), f32),
            pltpu.VMEM((n_tm, part, LANES), f32),
            pltpu.VMEM((n_scan, n_tm, part, LANES), f32),
            pltpu.VMEM((2, EDGE, LANES), f32),
            pltpu.VMEM((2, EDGE, LANES), f32),
            dma((len(tables),)),
            dma((4, n_tm)),
            dma((4, n_tm)),
            dma((2, 3, n_tm)),
            dma((2, 3, n_tm)),
        ],
        compiler_params=pltpu.CompilerParams(
            collective_id=2, has_side_effects=True, vmem_limit_bytes=56 * 2**20
        ),
        name="transform",
    )(spec, *tables)


def general_transform(spec_grad):
    n_tm = lax.axis_size("tm")
    tm_index = lax.axis_index("tm")
    windows = spec_grad.shape[0]
    stretch = spec_grad.shape[2]
    total = N1 * N2
    rows_f2 = N2 // n_tm
    rows_f1 = N1 // n_tm
    local = spec_grad.reshape(windows, 2, rows_f2, N1)
    moved = lax.all_to_all(local, "tm", split_axis=3, concat_axis=2, tiled=True)
    freq_two = jnp.arange(N2, dtype=jnp.int32)
    freq_one = tm_index * rows_f1 + jnp.arange(rows_f1, dtype=jnp.int32)
    time_two = jnp.arange(N2, dtype=jnp.int32)
    phase_two = angles(freq_two, time_two, N2)
    cos_two = jnp.cos(phase_two)
    sin_two = jnp.sin(phase_two)
    real_in = moved[:, 0]
    imag_in = moved[:, 1]
    part_re = jnp.einsum("wfa,ft->wat", real_in, cos_two, precision=high) - jnp.einsum(
        "wfa,ft->wat", imag_in, sin_two, precision=high
    )
    part_im = jnp.einsum("wfa,ft->wat", real_in, sin_two, precision=high) + jnp.einsum(
        "wfa,ft->wat", imag_in, cos_two, precision=high
    )
    twiddle = angles(freq_one, time_two, total)
    cos_tw = jnp.cos(twiddle)[None]
    sin_tw = jnp.sin(twiddle)[None]
    turned = jnp.stack(
        [part_re * cos_tw - part_im * sin_tw, part_re * sin_tw + part_im * cos_tw], 1
    )
    columns = lax.all_to_all(turned, "tm", split_axis=3, concat_axis=2, tiled=True)
    all_one = jnp.arange(N1, dtype=jnp.int32)
    phase_one = angles(all_one, all_one, N1)
    rows_out = jnp.einsum("wfb,ft->wbt", columns[:, 0], jnp.cos(phase_one), precision=high)
    rows_out = rows_out - jnp.einsum(
        "wfb,ft->wbt", columns[:, 1], jnp.sin(phase_one), precision=high
    )
    rows_out = rows_out * total ** (-0.5)
    placed = lax.all_to_all(rows_out, "tm", split_axis=2, concat_axis=1, tiled=True)
    avg_grad = jnp.transpose(placed, (0, 2, 1)).reshape(windows, stretch)
    cells = padded(avg_grad, (("tm", 1),), EDGE * LANES).reshape(windows, -1, LANES)
    return jnp.pad(cells, ((0, 0), (0, 8), (0, 0)))


def on_device(spec_grad, transients, kernels, shifts, tiles):
    n_tm, n_scan = lax.axis_size("tm"), lax.axis_size("scan")
    windows = spec_grad.shape[0]
    if windows == 1 and n_scan == 4 and N2 // n_tm == LANES and N1 // 2 % (8 * n_tm * n_scan) == 0:
        cells = transform(spec_grad.reshape(2 * LANES, N1), n_tm, n_scan)[None]
    else:
        cells = general_transform(spec_grad)
    table, scan_grad = None, []
    for w in range(windows):
        rows_w, table_w = scans_and_table(cells[w], transients[w], kernels, shifts[w], tiles[w])
        scan_grad.append(rows_w)
        table = table_w if table is None else table + table_w
    scan_grad = jnp.stack(scan_grad)
    sizes = (n_tm, n_scan)
    if sizes[0] <= 8:
        table = sum_everywhere(table, sizes)
    else:
        table = lax.psum(table[:, :TAPS], ("tm", "scan"))
    return (scan_grad, table)


def solution(mesh):
    placed = (P(None, None, "tm"), P(None, "scan", "tm"), P(), P(None, "scan"), P(None, "scan"))
    return jax.shard_map(
        on_device,
        mesh=mesh,
        in_specs=placed,
        out_specs=(P(None, "scan", "tm"), P()),
        check_vma=False,
    )
```
